32 devices in a mesh: rep: 2 (over x), fsdp: 16 (over z, y, core).
Axes of the slice: x: 2, y: 2, z: 4, core: 2. Of those that a mesh axis runs over, the one named last changes fastest.
Arguments:
- hidden: bfloat16 [2, 4096, 256], P('rep', 'fsdp'), may hold values from -6 to 6
- global_w: float32 [256, 5120], P('fsdp'), may hold values from -0.375 to 0.375
- momentum: float32 [256, 5120], P('fsdp'), may hold values from -0.375 to 0.375
- inner: float32 [2, 256, 5120], P('rep', 'fsdp'), may hold values from -0.375 to 0.375
Outputs:
- global_new: float32 [256, 5120], P('fsdp')
- momentum_new: float32 [256, 5120], P('fsdp')
- projected: bfloat16 [2, 4096, 5120], P('rep', 'fsdp')
The draws below stay inside these ranges and needn't reach their ends.
All inputs are finite; a program needn't handle non-finite values.
Results may differ from the reference program's by a relative error of at most 0.0049.
Values may be sent and summed in bfloat16 or wider, within the bound.
A program may use at most 64 MiB of HBM per device.

```python
import jax
import jax.numpy as jnp

D = 5120
FF_WIN = 256
TOKENS = 4096
N_REP = 2


def levels(rng, extent, cuts, least, largest):
    level = 1.0
    for position, blocks in cuts:
        heights = jax.random.uniform(jax.random.fold_in(jax.random.fold_in(rng, 6), position), (blocks,), jnp.float32, least / len(cuts), largest / len(cuts))
        level = level * jnp.repeat(jnp.exp(heights), extent[position] // blocks).reshape((-1,) + (1,) * (len(extent) - 1 - position))
    return level


def bell_draw(rng, shape, deviation, bound, shards=(), kind=jnp.bfloat16):
    array = jax.random.normal(rng, shape, jnp.float32) * deviation
    if len(shards) > 0:
        array = levels(rng, shape, shards, -0.22, 0.18) * array
    return jnp.clip(array, min=-bound, max=bound).astype(kind)


def setup_inputs(seed: int = 0) -> dict:
    seeds = jax.random.split(jax.random.key(seed), 5)
    return {
        "hidden": bell_draw(seeds[0], (N_REP, TOKENS, FF_WIN), 1.0, 6.0, ((0, 2), (1, 16))),
        "global_w": bell_draw(seeds[1], (FF_WIN, D), FF_WIN ** -0.5, 0.375, ((0, 16),), jnp.float32),
        "momentum": bell_draw(seeds[2], (FF_WIN, D), FF_WIN ** -0.5, 0.375, ((0, 16),), jnp.float32),
        "inner": bell_draw(seeds[3], (N_REP, FF_WIN, D), FF_WIN ** -0.5, 0.375, ((0, 2), (1, 16)), jnp.float32),
    }


def reference(hidden, global_w, momentum, inner):
    drift = jnp.mean(global_w[None] - inner, axis=0)
    momentum_new = 0.9 * momentum + drift
    global_new = global_w - 0.7 * (drift + 0.9 * momentum_new)
    blended = (0.5 * inner + 0.5 * global_new[None]).astype(jnp.bfloat16)
    outs = []
    for index in range(N_REP):
        outs.append(jnp.dot(hidden[index], blended[index], preferred_element_type=jnp.float32).astype(jnp.bfloat16))
    return global_new, momentum_new, jnp.stack(outs)
```

```python
import functools

import jax
import jax.numpy as jnp
from jax import lax
from jax.experimental import pallas as pl
from jax.experimental.pallas import tpu as pltpu
from jax.sharding import PartitionSpec as P

CHUNK = 1024
FAST_FIRST = 1


def split_line(devices):
    chips = devices // 2
    long = 1
    while long * long < chips:
        long *= 2
    return long, chips // long


def ways(size):
    if size == 1:
        return []
    return [0] if size == 2 else [-1, 1]


def step(x, s):
    return 1 - x if s == 0 else x + s


def source(x, s, hops):
    return 1 - x if s == 0 else x - s * hops


def inside(x, size):
    return jnp.logical_and(x >= 0, x < size)


def guarded(size, x, body):
    if size == 2:
        body()
    else:
        pl.when(inside(x, size))(body)


def kernel(
    replicas, devices,
    hidden_hbm, global_hbm, moment_hbm, inner_hbm,
    global_out, moment_out, projected_out,
    hidden, weights, moment, inner, drifts, gathered, result, new_w, new_m,
    load_sem, store_sem, rep_send, rep_recv, line_send, twin_send, line_recv, twin_recv,
):
    rows, width = weights.shape
    cols = CHUNK if width % CHUNK == 0 else width
    count = width // cols
    long, short = split_line(devices)
    rep = lax.axis_index("rep")
    me = lax.axis_index("fsdp")
    core = lax.rem(me, 2)
    chip = lax.div(me, 2)
    place = (lax.div(chip, short), lax.rem(chip, short))
    sizes = (long, short)

    def index(a, b, c):
        return (a * short + b) * 2 + c

    def device_along(axis, s):
        spot = list(place)
        spot[axis] = step(spot[axis], s)
        return index(spot[0], spot[1], core)

    twin = index(place[0], place[1], 1 - core)

    barrier = pltpu.get_barrier_semaphore()
    heard = jnp.int32(replicas)
    for other in range(1, replicas):
        pl.semaphore_signal(
            barrier, inc=1, device_id=(lax.rem(rep + other, replicas), me),
            device_id_type=pl.DeviceIdType.MESH,
        )
    pl.semaphore_signal(barrier, inc=1, device_id=(rep, twin), device_id_type=pl.DeviceIdType.MESH)
    for axis in range(2):
        for s in ways(sizes[axis]):
            def greet(axis=axis, s=s):
                pl.semaphore_signal(
                    barrier, inc=1, device_id=(rep, device_along(axis, s)),
                    device_id_type=pl.DeviceIdType.MESH,
                )
            spot = step(place[axis], s)
            guarded(sizes[axis], spot, greet)
            heard = heard + (1 if sizes[axis] == 2 else inside(spot, sizes[axis]).astype(jnp.int32))

    loads = [
        pltpu.make_async_copy(global_hbm, weights, load_sem.at[0]),
        pltpu.make_async_copy(inner_hbm.at[0], inner, load_sem.at[1]),
        pltpu.make_async_copy(moment_hbm, moment, load_sem.at[2]),
        pltpu.make_async_copy(hidden_hbm.at[0], hidden, load_sem.at[3]),
    ]
    for load in loads:
        load.start()
    loads[0].wait()
    loads[1].wait()
    drifts[rep] = (weights[...] - inner[...]).astype(jnp.bfloat16)
    pl.semaphore_wait(barrier, heard)

    def span(k):
        return pl.ds(k * cols, cols)

    for k in range(count):
        for other in range(1, replicas):
            part = drifts.at[rep, :, span(k)]
            pltpu.make_async_remote_copy(
                src_ref=part, dst_ref=part, send_sem=rep_send, recv_sem=rep_recv.at[k],
                device_id=(lax.rem(rep + other, replicas), me),
                device_id_type=pl.DeviceIdType.MESH,
            ).start()

    def slot(origin, k):
        return gathered.at[pl.ds(pl.multiple_of(origin * rows, rows), rows), span(k)]

    def fast(k):
        return 1 if k < FAST_FIRST else 0

    def send_line(origin, k, axis, s):
        def go():
            pltpu.make_async_remote_copy(
                src_ref=slot(origin, k), dst_ref=slot(origin, k),
                send_sem=line_send.at[fast(k), axis, 0 if s < 1 else 1],
                recv_sem=line_recv.at[origin, k],
                device_id=(rep, device_along(axis, s)), device_id_type=pl.DeviceIdType.MESH,
            ).start()
        guarded(sizes[axis], step(place[axis], s), go)

    def send_twin(origin, k):
        pltpu.make_async_remote_copy(
            src_ref=slot(origin, k), dst_ref=slot(origin, k),
            send_sem=twin_send, recv_sem=twin_recv.at[k],
            device_id=(rep, twin), device_id_type=pl.DeviceIdType.MESH,
        ).start()

    def await_line(origin, k):
        part = slot(origin, k)
        pltpu.make_async_copy(part, part, line_recv.at[origin, k]).wait()

    def origin_at(axis, x, y):
        return index(x, y, core) if axis == 0 else index(y, x, core)

    def own(k):
        part = drifts.at[0:replicas - 1, :, span(k)]
        pltpu.make_async_copy(part, part, rep_recv.at[k]).wait()
        total = drifts[0, :, span(k)].astype(jnp.float32)
        for other in range(1, replicas):
            total = total + drifts[other, :, span(k)].astype(jnp.float32)
        drift = total / replicas
        moved = 0.9 * moment[:, span(k)] + drift
        fresh = weights[:, span(k)] - 0.7 * (drift + 0.9 * moved)
        blended = (0.5 * inner[:, span(k)] + 0.5 * fresh).astype(jnp.bfloat16)
        gathered[pl.ds(pl.multiple_of(me * rows, rows), rows), span(k)] = blended
        first = fast(k)
        for axis in (first, 1 - first):
            for s in ways(sizes[axis]):
                send_line(me, k, axis, s)
        send_twin(me, k)
        new_m[:, span(k)] = moved
        new_w[:, span(k)] = fresh

    def first_line(k, hops):
        axis = fast(k)
        size = sizes[axis]
        if hops >= size:
            return
        for s in ways(size):
            x = source(place[axis], s, hops)
            def body(x=x, s=s):
                origin = origin_at(axis, x, place[1 - axis])
                await_line(origin, k)
                if s != 0:
                    send_line(origin, k, axis, s)
                for t in ways(sizes[1 - axis]):
                    send_line(origin, k, 1 - axis, t)
                send_twin(origin, k)
            guarded(size, x, body)

    def second_line(k, away, hops):
        axis = fast(k)
        size, other = sizes[axis], sizes[1 - axis]
        if away >= size or hops >= other:
            return
        sides = [0] if away == 0 else ([1] if size == 2 else [-away, away])
        for side in sides:
            x = place[axis] if away == 0 else (1 - place[axis] if size == 2 else place[axis] + side)
            def line(x=x):
                for s in ways(other):
                    y = source(place[1 - axis], s, hops)
                    def body(y=y, s=s):
                        origin = origin_at(axis, x, y)
                        await_line(origin, k)
                        if s != 0:
                            send_line(origin, k, 1 - axis, s)
                        send_twin(origin, k)
                    guarded(other, y, body)
            if away == 0:
                line()
            else:
                guarded(size, x, line)

    def multiply(k):
        part = gathered.at[0:devices // 2 * rows, span(k)]
        pltpu.make_async_copy(part, part, twin_recv.at[k]).wait()
        result[:, span(k)] = jnp.dot(
            hidden[...], gathered[:, span(k)], preferred_element_type=jnp.float32
        ).astype(jnp.bfloat16)
        pltpu.make_async_copy(
            result.at[:, span(k)], projected_out.at[0, :, span(k)], store_sem.at[2 + k]
        ).start()

    loads[2].wait()
    for k in range(count):
        own(k)
    stores = [
        pltpu.make_async_copy(new_w, global_out, store_sem.at[0]),
        pltpu.make_async_copy(new_m, moment_out, store_sem.at[1]),
    ]
    for store in stores:
        store.start()
    loads[3].wait()

    rounds = [[] for _ in range(2 * (long + short))]
    for k in range(count):
        axis = fast(k)
        for away in range(sizes[axis]):
            if away > 0:
                rounds[away].append((k, functools.partial(first_line, k, away)))
            for hops in range(1, sizes[1 - axis]):
                rounds[away + hops].append((k, functools.partial(second_line, k, away, hops)))
    last = [0] * count
    for number, events in enumerate(rounds):
        for k, _ in events:
            last[k] = number
    for number, events in enumerate(rounds):
        events.sort(key=lambda event: event[0])
        for place_in, (k, event) in enumerate(events):
            event()
            if number == last[k] and k not in [j for j, _ in events[place_in + 1:]]:
                multiply(k)

    def drain(sem, blocks, columns):
        part = gathered.at[0:blocks * rows, 0:columns]
        pltpu.make_async_copy(part, part, sem).wait()

    for other in range(1):
        part = drifts.at[0:replicas - 1]
        pltpu.make_async_copy(part, part, rep_send).wait()
    drain(twin_send, devices // 2, width)
    fast_columns = min(FAST_FIRST, count) * cols
    for kind, columns in ((0, width - fast_columns), (1, fast_columns)):
        if columns == 0:
            continue
        for axis in range(2):
            lines = 1 if axis == kind else sizes[1 - axis]
            size, x = sizes[axis], place[axis]
            for s in ways(size):
                sem = line_send.at[kind, axis, 0 if s < 1 else 1]
                if s == 0:
                    drain(sem, lines, columns)
                    continue
                for blocks in range(1, size):
                    at = blocks - 1 if s == 1 else size - blocks
                    pl.when(x == at)(functools.partial(drain, sem, blocks * lines, columns))
    for store in stores:
        store.wait()
    for k in range(count):
        pltpu.make_async_copy(
            result.at[:, span(k)], projected_out.at[0, :, span(k)], store_sem.at[2 + k]
        ).wait()


def shards(replicas, devices, hidden, global_w, momentum, inner):
    _, tokens, units = hidden.shape
    rows, width = global_w.shape
    count = width // CHUNK if width % CHUNK == 0 else 1
    f32, bf16 = jnp.float32, jnp.bfloat16
    dma = pltpu.SemaphoreType.DMA
    room = rows * width * (4 * 5 + 2 * replicas) + units * width * 2 + tokens * (width + units) * 2
    return pl.pallas_call(
        functools.partial(kernel, replicas, devices),
        out_shape=(
            jax.ShapeDtypeStruct((rows, width), f32),
            jax.ShapeDtypeStruct((rows, width), f32),
            jax.ShapeDtypeStruct((1, tokens, width), bf16),
        ),
        in_specs=[pl.BlockSpec(memory_space=pl.ANY)] * 4,
        out_specs=[pl.BlockSpec(memory_space=pl.ANY)] * 3,
        scratch_shapes=[
            pltpu.VMEM((tokens, units), bf16),
            pltpu.VMEM((rows, width), f32),
            pltpu.VMEM((rows, width), f32),
            pltpu.VMEM((rows, width), f32),
            pltpu.VMEM((replicas, rows, width), bf16),
            pltpu.VMEM((units, width), bf16),
            pltpu.VMEM((tokens, width), bf16),
            pltpu.VMEM((rows, width), f32),
            pltpu.VMEM((rows, width), f32),
            dma((4,)),
            dma((2 + count,)),
            dma,
            dma((count,)),
            dma((2, 2, 2)),
            dma,
            dma((devices, count)),
            dma((count,)),
        ],
        compiler_params=pltpu.CompilerParams(
            collective_id=0, has_side_effects=True, vmem_limit_bytes=room + (8 << 20)
        ),
        cost_estimate=pl.CostEstimate(
            flops=2 * tokens * units * width,
            bytes_accessed=rows * width * 20 + tokens * width * 2,
            transcendentals=0,
        ),
    )(hidden, global_w, momentum, inner)


def solution(mesh):
    in_specs = (P("rep", "fsdp", None), P("fsdp", None), P("fsdp", None), P("rep", "fsdp", None))
    out_specs = (P("fsdp", None), P("fsdp", None), P("rep", "fsdp", None))
    body = functools.partial(shards, mesh.shape["rep"], mesh.shape["fsdp"])
    return jax.shard_map(body, mesh=mesh, in_specs=in_specs, out_specs=out_specs, check_vma=False)
```

```python
import functools

import jax
import jax.numpy as jnp
from jax import lax
from jax.experimental import pallas as pl
from jax.experimental.pallas import tpu as pltpu
from jax.sharding import PartitionSpec as P

CUTS = (1,)
LAG = 0.0
RELEASE = 0.0
FAST = 0


def split_line(devices):
    chips = devices // 2
    long = 1
    while long * long < chips:
        long *= 2
    return long, chips // long


def ways(size):
    if size == 1:
        return []
    return [0] if size == 2 else [-1, 1]


def step(x, s):
    return 1 - x if s == 0 else x + s


def source(x, s, hops):
    return 1 - x if s == 0 else x - s * hops


def inside(x, size):
    return jnp.logical_and(x >= 0, x < size)


def guarded(size, x, body):
    if size == 2:
        body()
    else:
        pl.when(inside(x, size))(body)


def cut(width):
    total, starts, widths = sum(CUTS), [], []
    for number in range(len(CUTS)):
        at, end = (width * sum(CUTS[:number + more]) // total // 128 * 128 for more in (0, 1))
        starts.append(at)
        widths.append((width if number + 1 == len(CUTS) else end) - at)
    return starts, widths


def kernel(
    replicas, devices,
    hidden_hbm, global_hbm, moment_hbm, inner_hbm,
    new_w, new_m, result,
    hidden, weights, moment, inner, drifts, gathered,
    load_sem, rep_send, rep_recv, line_send, twin_send, line_recv, twin_recv,
):
    rows, width = weights.shape
    starts, widths = cut(width)
    count = len(widths)
    long, short = split_line(devices)
    rep = lax.axis_index("rep")
    me = lax.axis_index("fsdp")
    core = lax.rem(me, 2)
    chip = lax.div(me, 2)
    place = (lax.div(chip, short), lax.rem(chip, short))
    sizes = (long, short)

    def index(a, b, c):
        return (a * short + b) * 2 + c

    def device_along(axis, s):
        spot = list(place)
        spot[axis] = step(spot[axis], s)
        return index(spot[0], spot[1], core)

    twin = index(place[0], place[1], 1 - core)

    barrier = pltpu.get_barrier_semaphore()
    heard = jnp.int32(replicas)
    for other in range(1, replicas):
        pl.semaphore_signal(
            barrier, inc=1, device_id=(lax.rem(rep + other, replicas), me),
            device_id_type=pl.DeviceIdType.MESH,
        )
    pl.semaphore_signal(barrier, inc=1, device_id=(rep, twin), device_id_type=pl.DeviceIdType.MESH)
    for axis in range(2):
        for s in ways(sizes[axis]):
            def greet(axis=axis, s=s):
                pl.semaphore_signal(
                    barrier, inc=1, device_id=(rep, device_along(axis, s)),
                    device_id_type=pl.DeviceIdType.MESH,
                )
            spot = step(place[axis], s)
            guarded(sizes[axis], spot, greet)
            heard = heard + (1 if sizes[axis] == 2 else inside(spot, sizes[axis]).astype(jnp.int32))

    loads = [
        pltpu.make_async_copy(global_hbm, weights, load_sem.at[0]),
        pltpu.make_async_copy(inner_hbm.at[0], inner, load_sem.at[1]),
        pltpu.make_async_copy(moment_hbm, moment, load_sem.at[2]),
        pltpu.make_async_copy(hidden_hbm.at[0], hidden, load_sem.at[3]),
    ]
    for load in loads:
        load.start()
    loads[0].wait()
    loads[1].wait()
    drifts[rep] = (weights[...] - inner[...]).astype(jnp.bfloat16)
    pl.semaphore_wait(barrier, heard)

    def span(k):
        return pl.ds(starts[k], widths[k])

    for k in range(count):
        for other in range(1, replicas):
            part = drifts.at[rep, :, span(k)]
            pltpu.make_async_remote_copy(
                src_ref=part, dst_ref=part, send_sem=rep_send, recv_sem=rep_recv.at[k],
                device_id=(lax.rem(rep + other, replicas), me),
                device_id_type=pl.DeviceIdType.MESH,
            ).start()

    def slot(origin, k):
        return gathered.at[pl.ds(pl.multiple_of(origin * rows, rows), rows), span(k)]

    def fast(k):
        return 1 if k >= count - FAST else 0

    def send_line(origin, k, axis, s):
        def go():
            pltpu.make_async_remote_copy(
                src_ref=slot(origin, k), dst_ref=slot(origin, k),
                send_sem=line_send.at[fast(k), axis, 0 if s < 1 else 1],
                recv_sem=line_recv.at[origin, k],
                device_id=(rep, device_along(axis, s)), device_id_type=pl.DeviceIdType.MESH,
            ).start()
        guarded(sizes[axis], step(place[axis], s), go)

    def send_twin(origin, k):
        pltpu.make_async_remote_copy(
            src_ref=slot(origin, k), dst_ref=slot(origin, k),
            send_sem=twin_send, recv_sem=twin_recv.at[k],
            device_id=(rep, twin), device_id_type=pl.DeviceIdType.MESH,
        ).start()

    def await_line(origin, k):
        part = slot(origin, k)
        pltpu.make_async_copy(part, part, line_recv.at[origin, k]).wait()

    def origin_at(axis, x, y):
        return index(x, y, core) if axis == 0 else index(y, x, core)

    def own(k):
        part = drifts.at[0:replicas - 1, :, span(k)]
        pltpu.make_async_copy(part, part, rep_recv.at[k]).wait()
        total = drifts[0, :, span(k)].astype(jnp.float32)
        for other in range(1, replicas):
            total = total + drifts[other, :, span(k)].astype(jnp.float32)
        drift = total / replicas
        moved = 0.9 * moment[:, span(k)] + drift
        fresh = weights[:, span(k)] - 0.7 * (drift + 0.9 * moved)
        blended = (0.5 * inner[:, span(k)] + 0.5 * fresh).astype(jnp.bfloat16)
        gathered[pl.ds(pl.multiple_of(me * rows, rows), rows), span(k)] = blended
        for axis in ((1,) if fast(k) else (0, 1)):
            for s in ways(sizes[axis]):
                send_line(me, k, axis, s)
        send_twin(me, k)
        new_m[:, span(k)] = moved
        new_w[:, span(k)] = fresh

    def first_line(k, hops):
        axis = fast(k)
        size = sizes[axis]
        if hops >= size:
            return
        for s in ways(size):
            x = source(place[axis], s, hops)
            def body(x=x, s=s):
                origin = origin_at(axis, x, place[1 - axis])
                await_line(origin, k)
                if s != 0:
                    send_line(origin, k, axis, s)
                if axis == 0:
                    for t in ways(sizes[1]):
                        send_line(origin, k, 1, t)
                send_twin(origin, k)
            guarded(size, x, body)

    def release(k):
        for y in range(short):
            for s in ways(long):
                send_line(index(place[0], y, core), k, 0, s)

    def second_line(k, away, hops):
        axis = fast(k)
        size, other = sizes[axis], sizes[1 - axis]
        if away >= size or hops >= other:
            return
        sides = [0] if away == 0 else ([1] if size == 2 else [-away, away])
        for side in sides:
            x = place[axis] if away == 0 else (1 - place[axis] if size == 2 else place[axis] + side)
            def line(x=x):
                for s in ways(other):
                    y = source(place[1 - axis], s, hops)
                    def body(y=y, s=s):
                        origin = origin_at(axis, x, y)
                        await_line(origin, k)
                        if s != 0:
                            send_line(origin, k, 1 - axis, s)
                        send_twin(origin, k)
                    guarded(other, y, body)
            if away == 0:
                line()
            else:
                guarded(size, x, line)

    def multiply(k):
        part = gathered.at[0:devices // 2 * rows, span(k)]
        pltpu.make_async_copy(part, part, twin_recv.at[k]).wait()
        result[:, span(k)] = jnp.dot(
            hidden[...], gathered[:, span(k)], preferred_element_type=jnp.float32
        ).astype(jnp.bfloat16)

    loads[2].wait()

    slow = count - FAST
    ends = [(start + size) / width for start, size in zip(starts, widths)]
    share = starts[slow] / width if FAST else 1.0
    delay = 0.5
    events = []
    for k in range(count):
        if fast(k):
            part = ends[k] - share
            events.append((part / 2, k, functools.partial(own, k)))
            for hops in range(1, short):
                events.append((part + delay * hops, k, functools.partial(first_line, k, hops)))
            events.append((share * (long - 2) + part + RELEASE, k, functools.partial(release, k)))
            for away in range(short):
                for hops in range(1, long):
                    at = share * (long - 1) + short * ((1 - share) * (hops - 1) + part) + delay
                    events.append((at + 0.01 * away, k, functools.partial(second_line, k, away, hops)))
            continue
        part = ends[k]
        events.append((1 - share + part, k, functools.partial(own, k)))
        for away in range(long):
            if away > 0:
                at = share * (away - 1) + part + delay
                events.append((at, k, functools.partial(first_line, k, away)))
            for hops in range(1, short):
                at = 1 - share + share * (away + hops - 1) + part + delay * (1 if away == 0 else 2) + LAG
                events.append((at, k, functools.partial(second_line, k, away, hops)))
    events.sort(key=lambda event: event[0])
    final = {k: number for number, (_, k, _) in enumerate(events)}
    owns = count
    for number, (_, k, event) in enumerate(events):
        event()
        if event.func is own:
            owns -= 1
            if owns == 0:
                loads[3].wait()
        if number == final[k]:
            multiply(k)

    def drain(sem, blocks, columns):
        part = gathered.at[0:blocks * rows, 0:columns]
        pltpu.make_async_copy(part, part, sem).wait()

    for other in range(1):
        part = drifts.at[0:replicas - 1]
        pltpu.make_async_copy(part, part, rep_send).wait()
    drain(twin_send, devices // 2, width)
    fast_columns = sum(widths[count - FAST:]) if FAST else 0
    for kind, columns in ((0, width - fast_columns), (1, fast_columns)):
        if columns == 0:
            continue
        for axis in range(2):
            lines = 1 if axis == kind else sizes[1 - axis]
            size, x = sizes[axis], place[axis]
            for s in ways(size):
                sem = line_send.at[kind, axis, 0 if s < 1 else 1]
                if s == 0:
                    drain(sem, lines, columns)
                    continue
                for blocks in range(1, size):
                    at = blocks - 1 if s == 1 else size - blocks
                    pl.when(x == at)(functools.partial(drain, sem, blocks * lines, columns))


def shards(replicas, devices, hidden, global_w, momentum, inner):
    _, tokens, units = hidden.shape
    rows, width = global_w.shape
    count = len(CUTS)
    f32, bf16 = jnp.float32, jnp.bfloat16
    dma = pltpu.SemaphoreType.DMA
    room = rows * width * (4 * 5 + 2 * replicas) + units * width * 2 + tokens * (width + units) * 2
    hidden, global_w, momentum, inner = [
        pltpu.with_memory_space_constraint(x, pltpu.HBM) for x in (hidden, global_w, momentum, inner)
    ]
    fresh, moved, product = pl.pallas_call(
        functools.partial(kernel, replicas, devices),
        out_shape=(
            jax.ShapeDtypeStruct((rows, width), f32),
            jax.ShapeDtypeStruct((rows, width), f32),
            jax.ShapeDtypeStruct((tokens, width), bf16),
        ),
        in_specs=[pl.BlockSpec(memory_space=pltpu.HBM)] * 4,
        out_specs=[pl.BlockSpec(memory_space=pltpu.VMEM)] * 3,
        scratch_shapes=[
            pltpu.VMEM((tokens, units), bf16),
            pltpu.VMEM((rows, width), f32),
            pltpu.VMEM((rows, width), f32),
            pltpu.VMEM((rows, width), f32),
            pltpu.VMEM((replicas, rows, width), bf16),
            pltpu.VMEM((units, width), bf16),
            dma((4,)),
            dma,
            dma((count,)),
            dma((2, 2, 2)),
            dma,
            dma((devices, count)),
            dma((count,)),
        ],
        compiler_params=pltpu.CompilerParams(
            collective_id=0, has_side_effects=True, vmem_limit_bytes=room + (8 << 20)
        ),
        cost_estimate=pl.CostEstimate(
            flops=2 * tokens * units * width,
            bytes_accessed=rows * width * 20 + tokens * width * 2,
            transcendentals=0,
        ),
    )(hidden, global_w, momentum, inner)
    fresh, moved, product = [
        pltpu.with_memory_space_constraint(x, pltpu.VMEM) for x in (fresh, moved, product)
    ]
    outs = pl.pallas_call(
        write_out,
        out_shape=[jax.ShapeDtypeStruct(x.shape, x.dtype) for x in (fresh, moved, product)],
        in_specs=[pl.BlockSpec(memory_space=pltpu.VMEM)] * 3,
        out_specs=[pl.BlockSpec(memory_space=pl.ANY)] * 3,
        scratch_shapes=[dma((3,))],
    )(fresh, moved, product)
    return outs[0], outs[1], outs[2][None]


def write_out(*refs):
    half = len(refs) // 2
    copies = [
        pltpu.make_async_copy(source_ref, target, refs[-1].at[number])
        for number, (source_ref, target) in enumerate(zip(refs[:half], refs[half:-1]))
    ]
    for copy in copies:
        copy.start()
    for copy in copies:
        copy.wait()


def solution(mesh):
    in_specs = (P("rep", "fsdp", None), P("fsdp", None), P("fsdp", None), P("rep", "fsdp", None))
    out_specs = (P("fsdp", None), P("fsdp", None), P("rep", "fsdp", None))
    body = functools.partial(shards, mesh.shape["rep"], mesh.shape["fsdp"])
    return jax.shard_map(body, mesh=mesh, in_specs=in_specs, out_specs=out_specs, check_vma=False)
```

```python
import functools

import jax
import jax.numpy as jnp
from jax import lax
from jax.experimental import pallas as pl
from jax.experimental.pallas import tpu as pltpu
from jax.sharding import PartitionSpec as P

CUTS = (1,)
TILES = 5
LAG = 0.0
RELEASE = 0.0
FAST = 0


def split_line(devices):
    chips = devices // 2
    long = 1
    while long * long < chips:
        long *= 2
    return long, chips // long


def ways(size):
    if size == 1:
        return []
    return [0] if size == 2 else [-1, 1]


def step(x, s):
    return 1 - x if s == 0 else x + s


def source(x, s, hops):
    return 1 - x if s == 0 else x - s * hops


def inside(x, size):
    return jnp.logical_and(x >= 0, x < size)


def guarded(size, x, body):
    if size == 2:
        body()
    else:
        pl.when(inside(x, size))(body)


def cut(width):
    total, starts, widths = sum(CUTS), [], []
    for number in range(len(CUTS)):
        at, end = (width * sum(CUTS[:number + more]) // total // 128 * 128 for more in (0, 1))
        starts.append(at)
        widths.append((width if number + 1 == len(CUTS) else end) - at)
    return starts, widths


def kernel(
    replicas, devices,
    hidden_hbm, global_hbm, moment_hbm, inner_hbm,
    new_w, new_m, gathered, hidden,
    weights, moment, inner, drifts,
    load_sem, rep_send, rep_recv, line_send, twin_send, line_recv, twin_recv,
):
    rows, width = weights.shape
    starts, widths = cut(width)
    count = len(widths)
    long, short = split_line(devices)
    rep = lax.axis_index("rep")
    me = lax.axis_index("fsdp")
    core = lax.rem(me, 2)
    chip = lax.div(me, 2)
    place = (lax.div(chip, short), lax.rem(chip, short))
    sizes = (long, short)

    def index(a, b, c):
        return (a * short + b) * 2 + c

    def device_along(axis, s):
        spot = list(place)
        spot[axis] = step(spot[axis], s)
        return index(spot[0], spot[1], core)

    twin = index(place[0], place[1], 1 - core)

    barrier = pltpu.get_barrier_semaphore()
    heard = jnp.int32(replicas)
    for other in range(1, replicas):
        pl.semaphore_signal(
            barrier, inc=1, device_id=(lax.rem(rep + other, replicas), me),
            device_id_type=pl.DeviceIdType.MESH,
        )
    pl.semaphore_signal(barrier, inc=1, device_id=(rep, twin), device_id_type=pl.DeviceIdType.MESH)
    for axis in range(2):
        for s in ways(sizes[axis]):
            def greet(axis=axis, s=s):
                pl.semaphore_signal(
                    barrier, inc=1, device_id=(rep, device_along(axis, s)),
                    device_id_type=pl.DeviceIdType.MESH,
                )
            spot = step(place[axis], s)
            guarded(sizes[axis], spot, greet)
            heard = heard + (1 if sizes[axis] == 2 else inside(spot, sizes[axis]).astype(jnp.int32))

    loads = [
        pltpu.make_async_copy(global_hbm, weights, load_sem.at[0]),
        pltpu.make_async_copy(inner_hbm.at[0], inner, load_sem.at[1]),
        pltpu.make_async_copy(moment_hbm, moment, load_sem.at[2]),
        pltpu.make_async_copy(hidden_hbm.at[0], hidden, load_sem.at[3]),
    ]
    for load in loads:
        load.start()
    loads[0].wait()
    loads[1].wait()
    drifts[rep] = (weights[...] - inner[...]).astype(jnp.bfloat16)
    pl.semaphore_wait(barrier, heard)

    def span(k):
        return pl.ds(starts[k], widths[k])

    for k in range(count):
        for other in range(1, replicas):
            part = drifts.at[rep, :, span(k)]
            pltpu.make_async_remote_copy(
                src_ref=part, dst_ref=part, send_sem=rep_send, recv_sem=rep_recv.at[k],
                device_id=(lax.rem(rep + other, replicas), me),
                device_id_type=pl.DeviceIdType.MESH,
            ).start()

    def slot(origin, k):
        return gathered.at[pl.ds(pl.multiple_of(origin * rows, rows), rows), span(k)]

    def fast(k):
        return 1 if k >= count - FAST else 0

    def send_line(origin, k, axis, s):
        def go():
            pltpu.make_async_remote_copy(
                src_ref=slot(origin, k), dst_ref=slot(origin, k),
                send_sem=line_send.at[fast(k), axis, 0 if s < 1 else 1],
                recv_sem=line_recv.at[origin, k],
                device_id=(rep, device_along(axis, s)), device_id_type=pl.DeviceIdType.MESH,
            ).start()
        guarded(sizes[axis], step(place[axis], s), go)

    def send_twin(origin, k):
        pltpu.make_async_remote_copy(
            src_ref=slot(origin, k), dst_ref=slot(origin, k),
            send_sem=twin_send, recv_sem=twin_recv.at[k],
            device_id=(rep, twin), device_id_type=pl.DeviceIdType.MESH,
        ).start()

    def await_line(origin, k):
        part = slot(origin, k)
        pltpu.make_async_copy(part, part, line_recv.at[origin, k]).wait()

    def origin_at(axis, x, y):
        return index(x, y, core) if axis == 0 else index(y, x, core)

    def own(k):
        part = drifts.at[0:replicas - 1, :, span(k)]
        pltpu.make_async_copy(part, part, rep_recv.at[k]).wait()
        total = drifts[0, :, span(k)].astype(jnp.float32)
        for other in range(1, replicas):
            total = total + drifts[other, :, span(k)].astype(jnp.float32)
        drift = total / replicas
        moved = 0.9 * moment[:, span(k)] + drift
        fresh = weights[:, span(k)] - 0.7 * (drift + 0.9 * moved)
        blended = (0.5 * inner[:, span(k)] + 0.5 * fresh).astype(jnp.bfloat16)
        gathered[pl.ds(pl.multiple_of(me * rows, rows), rows), span(k)] = blended
        for axis in ((1,) if fast(k) else (0, 1)):
            for s in ways(sizes[axis]):
                send_line(me, k, axis, s)
        send_twin(me, k)
        new_m[:, span(k)] = moved
        new_w[:, span(k)] = fresh

    def first_line(k, hops):
        axis = fast(k)
        size = sizes[axis]
        if hops >= size:
            return
        for s in ways(size):
            x = source(place[axis], s, hops)
            def body(x=x, s=s):
                origin = origin_at(axis, x, place[1 - axis])
                await_line(origin, k)
                if s != 0:
                    send_line(origin, k, axis, s)
                if axis == 0:
                    for t in ways(sizes[1]):
                        send_line(origin, k, 1, t)
                send_twin(origin, k)
            guarded(size, x, body)

    def release(k):
        for y in range(short):
            for s in ways(long):
                send_line(index(place[0], y, core), k, 0, s)

    def second_line(k, away, hops):
        axis = fast(k)
        size, other = sizes[axis], sizes[1 - axis]
        if away >= size or hops >= other:
            return
        sides = [0] if away == 0 else ([1] if size == 2 else [-away, away])
        for side in sides:
            x = place[axis] if away == 0 else (1 - place[axis] if size == 2 else place[axis] + side)
            def line(x=x):
                for s in ways(other):
                    y = source(place[1 - axis], s, hops)
                    def body(y=y, s=s):
                        origin = origin_at(axis, x, y)
                        await_line(origin, k)
                        if s != 0:
                            send_line(origin, k, 1 - axis, s)
                        send_twin(origin, k)
                    guarded(other, y, body)
            if away == 0:
                line()
            else:
                guarded(size, x, line)

    def complete(k):
        part = gathered.at[0:devices // 2 * rows, span(k)]
        pltpu.make_async_copy(part, part, twin_recv.at[k]).wait()

    loads[2].wait()

    slow = count - FAST
    ends = [(start + size) / width for start, size in zip(starts, widths)]
    share = starts[slow] / width if FAST else 1.0
    delay = 0.5
    events = []
    for k in range(count):
        if fast(k):
            part = ends[k] - share
            events.append((part / 2, k, functools.partial(own, k)))
            for hops in range(1, short):
                events.append((part + delay * hops, k, functools.partial(first_line, k, hops)))
            events.append((share * (long - 2) + part + RELEASE, k, functools.partial(release, k)))
            for away in range(short):
                for hops in range(1, long):
                    at = share * (long - 1) + short * ((1 - share) * (hops - 1) + part) + delay
                    events.append((at + 0.01 * away, k, functools.partial(second_line, k, away, hops)))
            continue
        part = ends[k]
        events.append((1 - share + part, k, functools.partial(own, k)))
        for away in range(long):
            if away > 0:
                at = share * (away - 1) + part + delay
                events.append((at, k, functools.partial(first_line, k, away)))
            for hops in range(1, short):
                at = 1 - share + share * (away + hops - 1) + part + delay * (1 if away == 0 else 2) + LAG
                events.append((at, k, functools.partial(second_line, k, away, hops)))
    events.sort(key=lambda event: event[0])
    final = {k: number for number, (_, k, _) in enumerate(events)}
    owns = count
    for number, (_, k, event) in enumerate(events):
        event()
        if event.func is own:
            owns -= 1
            if owns == 0:
                loads[3].wait()
        if number == final[k]:
            complete(k)

    def drain(sem, blocks, columns):
        part = gathered.at[0:blocks * rows, 0:columns]
        pltpu.make_async_copy(part, part, sem).wait()

    for other in range(1):
        part = drifts.at[0:replicas - 1]
        pltpu.make_async_copy(part, part, rep_send).wait()
    drain(twin_send, devices // 2, width)
    fast_columns = sum(widths[count - FAST:]) if FAST else 0
    for kind, columns in ((0, width - fast_columns), (1, fast_columns)):
        if columns == 0:
            continue
        for axis in range(2):
            lines = 1 if axis == kind else sizes[1 - axis]
            size, x = sizes[axis], place[axis]
            for s in ways(size):
                sem = line_send.at[kind, axis, 0 if s < 1 else 1]
                if s == 0:
                    drain(sem, lines, columns)
                    continue
                for blocks in range(1, size):
                    at = blocks - 1 if s == 1 else size - blocks
                    pl.when(x == at)(functools.partial(drain, sem, blocks * lines, columns))


def shards(replicas, devices, hidden, global_w, momentum, inner):
    _, tokens, units = hidden.shape
    rows, width = global_w.shape
    count = len(CUTS)
    f32, bf16 = jnp.float32, jnp.bfloat16
    dma = pltpu.SemaphoreType.DMA
    room = rows * width * (4 * 5 + 2 * replicas) + units * width * 2 + tokens * (width + units) * 2
    hidden, global_w, momentum, inner = [
        pltpu.with_memory_space_constraint(x, pltpu.HBM) for x in (hidden, global_w, momentum, inner)
    ]
    held = pl.pallas_call(
        functools.partial(kernel, replicas, devices),
        out_shape=(
            jax.ShapeDtypeStruct((rows, width), f32),
            jax.ShapeDtypeStruct((rows, width), f32),
            jax.ShapeDtypeStruct((units, width), bf16),
            jax.ShapeDtypeStruct((tokens, units), bf16),
        ),
        in_specs=[pl.BlockSpec(memory_space=pltpu.HBM)] * 4,
        out_specs=[pl.BlockSpec(memory_space=pltpu.VMEM)] * 4,
        scratch_shapes=[
            pltpu.VMEM((rows, width), f32),
            pltpu.VMEM((rows, width), f32),
            pltpu.VMEM((rows, width), f32),
            pltpu.VMEM((replicas, rows, width), bf16),
            dma((4,)),
            dma,
            dma((count,)),
            dma((2, 2, 2)),
            dma,
            dma((devices, count)),
            dma((count,)),
        ],
        compiler_params=pltpu.CompilerParams(
            collective_id=0, has_side_effects=True, vmem_limit_bytes=room + (8 << 20)
        ),
        cost_estimate=pl.CostEstimate(
            flops=2 * tokens * units * width,
            bytes_accessed=rows * width * 20 + tokens * width * 2,
            transcendentals=0,
        ),
    )(hidden, global_w, momentum, inner)
    held = [pltpu.with_memory_space_constraint(x, pltpu.VMEM) for x in held]
    outs = pl.pallas_call(
        write_out,
        out_shape=(
            jax.ShapeDtypeStruct((rows, width), f32),
            jax.ShapeDtypeStruct((rows, width), f32),
            jax.ShapeDtypeStruct((tokens, width), bf16),
        ),
        in_specs=[pl.BlockSpec(memory_space=pltpu.VMEM)] * 4,
        out_specs=[pl.BlockSpec(memory_space=pl.ANY)] * 3,
        scratch_shapes=[pltpu.VMEM((tokens, width), bf16), dma((2 + TILES,))],
        compiler_params=pltpu.CompilerParams(vmem_limit_bytes=room + (8 << 20)),
    )(*held)
    return outs[0], outs[1], outs[2][None]


def write_out(new_w, new_m, gathered, hidden, global_out, moment_out, projected_out, result, sem):
    copies = [
        pltpu.make_async_copy(new_w, global_out, sem.at[0]),
        pltpu.make_async_copy(new_m, moment_out, sem.at[1]),
    ]
    for copy in copies:
        copy.start()
    tile = gathered.shape[1] // TILES
    for number in range(TILES):
        span = pl.ds(number * tile, tile)
        result[:, span] = jnp.dot(
            hidden[...], gathered[:, span], preferred_element_type=jnp.float32
        ).astype(jnp.bfloat16)
        copies.append(
            pltpu.make_async_copy(result.at[:, span], projected_out.at[:, span], sem.at[2 + number])
        )
        copies[-1].start()
    for copy in copies:
        copy.wait()


def solution(mesh):
    in_specs = (P("rep", "fsdp", None), P("fsdp", None), P("fsdp", None), P("rep", "fsdp", None))
    out_specs = (P("fsdp", None), P("fsdp", None), P("rep", "fsdp", None))
    body = functools.partial(shards, mesh.shape["rep"], mesh.shape["fsdp"])
    return jax.shard_map(body, mesh=mesh, in_specs=in_specs, out_specs=out_specs, check_vma=False)
```
